128 devices in a mesh: grp: 8 (over z, core), sub: 16 (over y, x).
Axes of the slice: x: 4, y: 4, z: 4, core: 2. Of those that a mesh axis runs over, the one named last changes fastest.
Arguments:
- points: bfloat16 [32768, 1024], P(('grp', 'sub')), may hold values from -20 to 20
- fine_initial: float32 [131072, 1024], P(('grp', 'sub')), may hold values from -6 to 6
- coarse_initial: float32 [16384, 1024], P('sub'), may hold values from -6 to 6
- assign: int32 [2, 32768], P(None, ('grp', 'sub')), may hold values from 0 to 131071, as said below
- parent: int32 [131072], P(('grp', 'sub')), may hold values from 0 to 16383, as said below
Outputs:
- fine_centroids: float32 [131072, 1024], P(('grp', 'sub'))
- coarse_centroids: float32 [16384, 1024], P('sub')
The draws below stay inside these ranges and needn't reach their ends.
Inputs may be any that keep to these rules, and one draw needn't show every extreme that they name: `assign`: Level-1 centroid k is held by device k // 1024, devices counted in the order grp+sub. In each iteration, among the 256 points of one device at most 4 name centroids held by one device, and some devices receive exactly 4 points from every device. `parent`: Level-2 centroid m lies at sub index m // 1024, in share (m % 1024) // 128 of it. Among the 1024 level-1 centroids of one device at most 128 have parents at one sub index and at most 16 in one share; at every grp index some sub indices receive exactly 128 from every device of that grp index, exactly 16 in each of their shares.
All inputs are finite; a program needn't handle non-finite values.
Results may differ from the reference program's by a relative error of at most 0.0037.
Values may be sent and summed in bfloat16 or wider, within the bound.
No kernel may reach another device: no remote copies, remote signals or barrier semaphores. Data moves between devices by JAX's collectives and lax.ppermute only.
A program may use at most 128 MiB of HBM per device.

```python
import math
import jax
import jax.numpy as jnp
from jax import lax

D = 1024
NP_DEV = 256
K1_DEV = 1024
K2_DEV = 1024
ITER1 = 2
ITER2 = 2
NPTS = 32768
K1 = 131072
K2 = 16384
CAP = 4
NHOT = 16
CAP2 = 128
NHOT2 = 4
SHARE2 = 128
N_GRP = 8
N_SUB = 16
DEVICES = 128


def spread_ranked(base_key, blocks, rows, owners, hot_count, capacity, group):

    def one_block(block_index):
        order = jax.random.permutation(jax.random.fold_in(base_key, block_index // group), owners)
        slots = jnp.arange(rows, dtype=jnp.int32)
        cold_count = owners - hot_count
        hot_pick = jnp.minimum(slots // capacity, hot_count - 1)
        hot_rank = slots % capacity
        cold_slot = jnp.maximum(slots - hot_count * capacity, 0)
        cold_pick = hot_count + cold_slot % cold_count
        cold_rank = cold_slot // cold_count
        is_hot = slots < hot_count * capacity
        pick = jnp.where(is_hot, hot_pick, cold_pick)
        rank = jnp.where(is_hot, hot_rank, cold_rank)
        shuffle = jax.random.permutation(jax.random.fold_in(jax.random.fold_in(base_key, 977), block_index), rows)
        return (order[pick][shuffle], rank[shuffle])
    return jax.vmap(one_block)(jnp.arange(blocks, dtype=jnp.int32))


def draw_points(key, part):
    key = jax.random.fold_in(key, 7)
    column_scale = jnp.exp(jax.random.uniform(jax.random.fold_in(key, 1), (D,), jnp.float32, -1.2, 1.2))
    row_scale = jnp.exp(jax.random.uniform(jax.random.fold_in(key, 2), (NPTS, 1), jnp.float32, -0.7, 0.7))
    base = jax.random.normal(jax.random.fold_in(key, 3), (NPTS, D), jnp.float32)
    return jnp.clip(base * column_scale * row_scale, -20.0, 20.0).astype(jnp.bfloat16)


def draw_assign(key, part):
    key = jax.random.fold_in(key, 3)
    layers = []
    for iteration in range(ITER1):
        iter_key = jax.random.fold_in(key, iteration)
        owner, ranks = spread_ranked(jax.random.fold_in(iter_key, 1), DEVICES, NP_DEV, DEVICES, NHOT, CAP, DEVICES)
        local = jax.random.randint(jax.random.fold_in(iter_key, 2), (DEVICES, NP_DEV), 0, K1_DEV, dtype=jnp.int32)
        layers.append((owner * K1_DEV + local).reshape(NPTS))
    return jnp.stack(layers)


def draw_parent(key, part):
    key = jax.random.fold_in(key, 5)
    owner, ranks = spread_ranked(jax.random.fold_in(key, 1), DEVICES, K1_DEV, N_SUB, NHOT2, CAP2, N_SUB)
    share = ranks % N_GRP
    within = jax.random.randint(jax.random.fold_in(key, 2), (DEVICES, K1_DEV), 0, SHARE2, dtype=jnp.int32)
    return (owner * K2_DEV + share * SHARE2 + within).reshape(K1)


def levels(own_key, dims, split, least, top_value):
    level, own = 1.0, jax.random.fold_in(own_key, 6)
    for position, parts in split:
        heights = jnp.exp(jax.random.uniform(jax.random.fold_in(own, position), (parts,), jnp.float32, least / len(split), top_value / len(split)))
        level = level * jnp.repeat(heights, dims[position] // parts).reshape([-1 if axis == position else 1 for axis in range(len(dims))])
    return level


def centred(own_key, shape, spread, bound, pieces=(), kind=jnp.bfloat16):
    gain = levels(own_key, shape, pieces, -0.22, 0.18) if pieces else 1.0
    entries = jax.random.normal(own_key, shape, jnp.float32) * spread * gain
    return jnp.minimum(jnp.maximum(entries, -bound), bound).astype(kind)


def setup_inputs(seed: int = 0) -> dict:
    key_list = jax.random.split(jax.random.key(seed), 6)
    return {
        "points": draw_points(jax.random.fold_in(key_list[5], 71), 0),
        "fine_initial": centred(key_list[1], (K1, D), 1.0, 6.0, ((0, 128),), jnp.float32),
        "coarse_initial": centred(key_list[2], (K2, D), 1.0, 6.0, ((0, 16),), jnp.float32),
        "assign": draw_assign(jax.random.fold_in(key_list[5], 71), 0),
        "parent": draw_parent(jax.random.fold_in(key_list[5], 71), 0),
    }


def lloyd_update(members, targets, centers, count):
    total_rows = members.shape[0]
    block_rows = math.gcd(total_rows, 2048)
    width = members.shape[1]

    def absorb(carry, block_index):
        sums_acc, mass_acc = carry
        start = block_index * block_rows
        rows_float = lax.dynamic_slice_in_dim(members, start, block_rows, 0).astype(jnp.float32)
        labels = lax.dynamic_slice_in_dim(targets, start, block_rows, 0)
        nearest = jnp.take(centers, labels, axis=0)
        distance = jnp.sum((rows_float - nearest) ** 2, axis=1) / width
        weights = 1.0 / (1.0 + distance)
        scaled = lax.optimization_barrier((weights[:, None] * rows_float).astype(jnp.bfloat16)).astype(jnp.float32)
        return (sums_acc.at[labels].add(scaled), mass_acc.at[labels].add(weights)), None

    initial = (jnp.zeros((count, width), jnp.float32), jnp.zeros((count,), jnp.float32))
    steps_total = total_rows // block_rows
    (sums_acc, mass_acc), _ = lax.scan(absorb, initial, jnp.arange(steps_total, dtype=jnp.int32))
    return (sums_acc + centers) / (mass_acc + 1.0)[:, None]


def reference(points, fine_initial, coarse_initial, assign, parent):
    level_one = fine_initial
    for iteration in range(ITER1):
        level_one = lloyd_update(points, assign[iteration], level_one, K1)
    rounded = lax.optimization_barrier(level_one.astype(jnp.bfloat16))
    level_two = coarse_initial
    for iteration in range(ITER2):
        level_two = lloyd_update(rounded, parent, level_two, K2)
    return level_one, level_two
```

```python
import jax
import jax.numpy as jnp
from jax import lax
from jax.experimental import pallas as pl
from jax.experimental.pallas import tpu as pltpu
from jax.sharding import PartitionSpec as P

ITER2 = 2
CAP = 4
CAP_SHARE = 16
EXTRA = 128
DIGIT = 32
F32 = jnp.float32
BF16 = jnp.bfloat16
VMEM_LIMIT = 56 * 1024 * 1024


def nt(a, b):
    return lax.dot_general(a, b, (((1,), (1,)), ((), ())), preferred_element_type=F32)


def tn(a, b):
    return lax.dot_general(a, b, (((0,), (0,)), ((), ())), preferred_element_type=F32)


def nn(a, b):
    return lax.dot_general(a, b, (((1,), (0,)), ((), ())), preferred_element_type=F32)


def iota(shape, dim):
    return lax.broadcasted_iota(jnp.int32, shape, dim)


def onehot(mask):
    return jnp.where(mask, 1.0, 0.0).astype(BF16)


def split2(x):
    hi = x.astype(BF16)
    lo = (x - hi.astype(F32)).astype(BF16)
    return hi, lo


def rank_in_bucket(dest, buckets):
    n = dest.shape[1]
    member = iota((buckets, n), 0) == dest
    earlier = onehot(iota((n, n), 0) < iota((n, n), 1))
    before = nn(onehot(member), earlier)
    return jnp.sum(jnp.where(member, before, 0.0), axis=0, keepdims=True).astype(jnp.int32)


def pack_one_kernel(devices, owned, share, subs, assign_ref, parent_ref, points_ref, out_ref, slot_ref):
    iters, n = assign_ref.shape
    slots = devices * CAP * iters
    width = points_ref.shape[1]
    group = CAP * iters
    hot = None
    extra = jnp.zeros((slots, EXTRA), F32)
    slot_iota = iota((slots, n), 0)
    for t in range(iters):
        target = assign_ref[t : t + 1, :]
        dest = target // owned
        local = target % owned
        rank = rank_in_bucket(dest, devices)
        slot = dest * group + t * CAP + rank
        mask = slot_iota == slot
        hot = mask if hot is None else jnp.logical_or(hot, mask)
        row = iota((EXTRA, n), 0)
        digits = jnp.where(row == 0, local // DIGIT + 1, jnp.where(row == 1, local % DIGIT, 0))
        extra = extra + nt(onehot(mask), digits.astype(F32).astype(BF16))
    out_ref[:, :width] = nn(onehot(hot), points_ref[...]).astype(BF16)
    parent = parent_ref[...]
    k = parent.shape[1]
    per_sub = share * (devices // subs)
    dest2 = (parent % per_sub) // share * subs + parent // per_sub
    local2 = parent % share
    rank2 = rank_in_bucket(dest2, devices)
    slot_ref[...] = dest2 * CAP_SHARE + rank2
    slot8 = dest2 * group + rank2 % group
    row = iota((EXTRA, k), 0)
    labels = jnp.where(row == 2 + rank2 // group, local2 + 1, 0)
    extra = extra + nt(onehot(iota((slots, k), 0) == slot8), labels.astype(F32).astype(BF16))
    out_ref[:, width:] = extra.astype(BF16)


def lloyd_one_kernel(iters, got_ref, centers_ref, slot_ref, out_ref, send_ref):
    owned, width = centers_ref.shape
    group = CAP * iters
    total = got_ref.shape[0]
    half = total // 2
    got = got_ref[...].astype(F32).reshape(total // 16, 16, width + EXTRA)
    even = got[:, 0:8, :].reshape(half, width + EXTRA)
    odd = got[:, 8:16, :].reshape(half, width + EXTRA)
    low = iota((half, width + EXTRA), 0) % 8 < CAP
    for t in range(iters):
        if t == 0:
            rows = jnp.where(low, even, pltpu.roll(odd, CAP, 0))
        else:
            rows = jnp.where(low, pltpu.roll(even, half - CAP, 0), odd)
        values = rows[:, :width]
        label = ((rows[:, width : width + 1] - 1.0) * DIGIT + rows[:, width + 1 : width + 2]).astype(jnp.int32)
        member = onehot(iota((half, owned), 1) == label)
        centers = centers_ref[...] if t == 0 else out_ref[...]
        hi, lo = split2(centers)
        nearest = nn(member, hi) + nn(member, lo)
        distance = jnp.sum((values - nearest) ** 2, axis=1, keepdims=True) / width
        weights = 1.0 / (1.0 + distance)
        scaled = (weights * values).astype(BF16)
        sums = tn(member, scaled)
        mass = tn(member, weight_columns(weights))
        scale = 1.0 / (jnp.sum(mass, axis=1, keepdims=True) + 1.0)
        out_ref[...] = (sums + centers) * scale
    rounded = out_ref[...].astype(BF16)
    slots = send_ref.shape[0]
    step = 512
    for s in range(0, slots, step):
        pick = onehot(iota((step, owned), 0) + s == slot_ref[...])
        send_ref[s : s + step, :] = nn(pick, rounded).astype(BF16)


def weight_columns(weights):
    n = weights.shape[0]
    hi = weights.astype(BF16).astype(F32)
    mid = (weights - hi).astype(BF16).astype(F32)
    low = weights - hi - mid
    lane = iota((n, 128), 1)
    cols = jnp.where(lane == 0, hi, jnp.where(lane == 1, mid, jnp.where(lane == 2, low, 0.0)))
    return cols.astype(BF16)


def lloyd_two_kernel(share_index_ref, got_ref, extra_ref, centers_ref, out_ref, member_ref, acc_ref, mass_ref):
    del share_index_ref
    share, width = centers_ref.shape
    total = got_ref.shape[0]
    extra = extra_ref[...].astype(F32)
    lane = iota((total // 2, share), 1)
    parts = []
    for j in range(2):
        label = extra[:, 2 + j : 3 + j].astype(jnp.int32) - 1
        parts.append(jnp.where(lane == label, 1.0, 0.0).reshape(total // 16, 8, share))
    member_ref[...] = jnp.concatenate(parts, axis=1).reshape(total, share).astype(BF16)
    centers = centers_ref[...]
    step = 256
    for _ in range(ITER2):
        hi, lo = split2(centers)
        acc_ref[...] = jnp.zeros_like(acc_ref)
        mass_ref[...] = jnp.zeros_like(mass_ref)

        def chunk(c, carry):
            at = pl.ds(pl.multiple_of(c * step, step), step)
            member = member_ref[at, :]
            values = got_ref[at, :].astype(F32)
            nearest = nn(member, hi) + nn(member, lo)
            distance = jnp.sum((values - nearest) ** 2, axis=1, keepdims=True) / width
            weights = 1.0 / (1.0 + distance)
            acc_ref[...] += tn(member, (weights * values).astype(BF16))
            mass_ref[...] += tn(member, weight_columns(weights))
            return carry

        lax.fori_loop(0, total // step, chunk, 0)
        scale = 1.0 / (jnp.sum(mass_ref[...], axis=1, keepdims=True) + 1.0)
        centers = (acc_ref[...] + centers) * scale
    out_ref[...] = centers.astype(BF16)


def assemble_kernel(order_ref, *refs):
    out_ref = refs[-1]
    rows = refs[0].shape[0]
    for i, ref in enumerate(refs[:-1]):
        at = pl.multiple_of(order_ref[i] * rows, rows)
        out_ref[pl.ds(at, rows), :] = ref[...].astype(F32)


def whole():
    return pl.BlockSpec(memory_space=pltpu.VMEM)


def params():
    return pltpu.CompilerParams(vmem_limit_bytes=VMEM_LIMIT)


def shards(points, fine_initial, coarse_initial, assign, parent):
    groups = lax.axis_size("grp")
    subs = lax.axis_size("sub")
    devices = groups * subs
    iters, n = assign.shape
    width = points.shape[1]
    owned = fine_initial.shape[0]
    share = coarse_initial.shape[0] // groups
    slots = devices * CAP * iters
    slots_two = devices * CAP_SHARE

    send, slot_two = pl.pallas_call(
        lambda *refs: pack_one_kernel(devices, owned, share, subs, *refs),
        out_shape=(
            jax.ShapeDtypeStruct((slots, width + EXTRA), BF16),
            jax.ShapeDtypeStruct((1, owned), jnp.int32),
        ),
        in_specs=[whole()] * 3,
        out_specs=(whole(), whole()),
        compiler_params=params(),
        name="pack_points",
    )(assign, parent.reshape(1, owned), points)
    got = lax.all_to_all(
        send.reshape(devices, CAP * iters, width + EXTRA), ("grp", "sub"), split_axis=0, concat_axis=0, tiled=True
    ).reshape(slots, width + EXTRA)

    fine, send_two = pl.pallas_call(
        lambda *refs: lloyd_one_kernel(iters, *refs),
        out_shape=(
            jax.ShapeDtypeStruct((owned, width), F32),
            jax.ShapeDtypeStruct((slots_two, width), BF16),
        ),
        in_specs=[whole()] * 3,
        out_specs=(whole(), whole()),
        compiler_params=params(),
        name="level_one",
    )(got, fine_initial, slot_two)
    got_two = lax.all_to_all(
        send_two.reshape(devices, CAP_SHARE, width), ("grp", "sub"), split_axis=0, concat_axis=0, tiled=True
    ).reshape(slots_two, width)

    me = lax.axis_index("grp")
    own = pl.pallas_call(
        lloyd_two_kernel,
        out_shape=jax.ShapeDtypeStruct((share, width), BF16),
        grid_spec=pltpu.PrefetchScalarGridSpec(
            num_scalar_prefetch=1,
            grid=(1,),
            in_specs=[
                pl.BlockSpec((slots_two, width), lambda i, s: (0, 0)),
                pl.BlockSpec((slots, EXTRA), lambda i, s: (0, width // EXTRA)),
                pl.BlockSpec((share, width), lambda i, s: (s[0], 0)),
            ],
            out_specs=pl.BlockSpec((share, width), lambda i, s: (0, 0)),
            scratch_shapes=[
                pltpu.VMEM((slots_two, share), BF16),
                pltpu.VMEM((share, width), F32),
                pltpu.VMEM((share, 128), F32),
            ],
        ),
        compiler_params=params(),
        name="level_two",
    )(me.astype(jnp.int32).reshape(1), got_two, got, coarse_initial)

    blocks = [own]
    for k in range(1, groups // 2):
        blocks.append(lax.ppermute(own, "grp", [(g, (g + 2 * k) % groups) for g in range(groups)]))
    blocks += [lax.ppermute(b, "grp", [(g, g ^ 1) for g in range(groups)]) for b in blocks]
    order = [(me - 2 * k) % groups for k in range(groups // 2)]
    order += [g ^ 1 for g in order]
    coarse = pl.pallas_call(
        assemble_kernel,
        out_shape=jax.ShapeDtypeStruct((groups * share, width), F32),
        in_specs=[pl.BlockSpec(memory_space=pltpu.SMEM)] + [whole()] * groups,
        out_specs=whole(),
        compiler_params=params(),
        name="assemble",
    )(jnp.stack(order).astype(jnp.int32), *blocks)
    return fine, coarse


def solution(mesh):
    return jax.shard_map(
        shards,
        mesh=mesh,
        in_specs=(
            P(("grp", "sub"), None),
            P(("grp", "sub"), None),
            P("sub", None),
            P(None, ("grp", "sub")),
            P(("grp", "sub")),
        ),
        out_specs=(P(("grp", "sub"), None), P("sub", None)),
        check_vma=False,
    )
```

```python
import jax
import jax.numpy as jnp
from jax import lax
from jax.experimental import pallas as pl
from jax.experimental.pallas import tpu as pltpu
from jax.sharding import PartitionSpec as P

ITER2 = 2
CAP = 4
CAP_SHARE = 16
EXTRA = 128
DIGIT = 32
F32 = jnp.float32
BF16 = jnp.bfloat16
TURNS = (2, 1, 3)
PACK_MIB = 16
ONE_MIB = 36
TWO_MIB = 24
PLACE_MIB = 16


def nt(a, b):
    return lax.dot_general(a, b, (((1,), (1,)), ((), ())), preferred_element_type=F32)


def tn(a, b):
    return lax.dot_general(a, b, (((0,), (0,)), ((), ())), preferred_element_type=F32)


def nn(a, b):
    return lax.dot_general(a, b, (((1,), (0,)), ((), ())), preferred_element_type=F32)


def iota(shape, dim):
    return lax.broadcasted_iota(jnp.int32, shape, dim)


def onehot(mask):
    return jnp.where(mask, 1.0, 0.0).astype(BF16)


def split2(x):
    hi = x.astype(BF16)
    lo = (x - hi.astype(F32)).astype(BF16)
    return hi, lo


def rank_in_bucket(member):
    n = member.shape[1]
    step = 128
    ones = jnp.where(member, 1.0, 0.0)
    earlier = onehot(iota((step, step), 0) < iota((step, step), 1))
    seen = jnp.zeros((member.shape[0], 1), F32)
    ranks = []
    for c in range(0, n, step):
        block = ones[:, c : c + step]
        before = nn(block.astype(BF16), earlier) + seen
        ranks.append(jnp.sum(block * before, axis=0, keepdims=True))
        seen = seen + jnp.sum(block, axis=1, keepdims=True)
    return jnp.concatenate(ranks, axis=1).astype(jnp.int32)


def pack_one_kernel(
    devices, owned, share, subs, assign_hbm, parent_hbm, points_hbm, out_ref, slot_ref, assign_ref, parent_ref, points_ref, sems
):
    copies = [
        pltpu.make_async_copy(parent_hbm, parent_ref, sems.at[0]),
        pltpu.make_async_copy(assign_hbm, assign_ref, sems.at[1]),
        pltpu.make_async_copy(points_hbm, points_ref, sems.at[2]),
    ]
    for copy in copies:
        copy.start()
    copies[0].wait()
    iters, n = assign_ref.shape
    group = CAP * iters
    slots = devices * group
    width = points_ref.shape[1]

    parent = parent_ref[...]
    k = parent.shape[1]
    per_sub = share * (devices // subs)
    dest = (parent % per_sub) // share * subs + parent // per_sub
    member = iota((devices, k), 0) == dest
    rank = rank_in_bucket(member)
    slot_ref[...] = dest * CAP_SHARE + rank
    lane = iota((EXTRA, k), 0)
    labels = jnp.where(lane == CAP_SHARE + rank, parent % share + 1, 0)
    labels = nt(onehot(member), labels.astype(F32).astype(BF16)).astype(BF16)
    spread = onehot(iota((slots, devices), 0) == iota((slots, devices), 1) * group)
    extra = nn(spread, labels)

    copies[1].wait()
    hot = None
    slot_iota = iota((slots, n), 0)
    for t in range(iters):
        target = assign_ref[t : t + 1, :]
        dest = target // owned
        local = target % owned
        rank = rank_in_bucket(iota((devices, n), 0) == dest)
        mask = slot_iota == dest * group + t * CAP + rank
        hot = mask if hot is None else jnp.logical_or(hot, mask)
        lane = iota((EXTRA, n), 0)
        digits = jnp.where(lane == 0, local // DIGIT + 1, jnp.where(lane == 1, local % DIGIT, 0))
        extra = extra + nt(onehot(mask), digits.astype(F32).astype(BF16))
    out_ref[:, width:] = extra.astype(BF16)
    copies[2].wait()
    out_ref[:, :width] = nn(onehot(hot), points_ref[...]).astype(BF16)


def lloyd_one_kernel(
    iters, index_ref, got_ref, centers_ref, slot_ref, coarse_hbm, out_hbm, send_ref, two_ref, share_ref, out_ref, scaled_ref, member_ref, sems
):
    share = share_ref.shape[0]
    start = pl.multiple_of(index_ref[0] * share, share)
    share_copy = pltpu.make_async_copy(coarse_hbm.at[pl.ds(start, share)], share_ref, sems.at[0])
    share_copy.start()
    owned, width = centers_ref.shape
    group = CAP * iters
    total = got_ref.shape[0]
    half = total // 2
    step = 128
    member_two(group, got_ref, two_ref)
    low = iota((step, EXTRA), 0) % 8 < CAP
    wide_low = iota((step, width), 0) % 8 < CAP
    for t in range(iters):
        old_ref = centers_ref if t == 0 else out_ref
        rounded = old_ref[...].astype(BF16)
        mass = jnp.zeros((owned, EXTRA), F32)
        for c in range(0, half, step):
            def rows(lo, hi, keep):
                got = got_ref[2 * c : 2 * (c + step), lo:hi].astype(F32).reshape(step // 8, 16, hi - lo)
                even = got[:, 0:8, :].reshape(step, hi - lo)
                odd = got[:, 8:16, :].reshape(step, hi - lo)
                if t == 0:
                    return jnp.where(keep, even, pltpu.roll(odd, CAP, 0))
                return jnp.where(keep, pltpu.roll(even, step - CAP, 0), odd)

            extra = rows(width, width + EXTRA, low)
            values = rows(0, width, wide_low)
            label = ((extra[:, 0:1] - 1.0) * DIGIT + extra[:, 1:2]).astype(jnp.int32)
            member = onehot(iota((step, owned), 1) == label)
            member_ref[c : c + step, :] = member
            nearest = nn(member, rounded)
            distance = jnp.sum((values - nearest) ** 2, axis=1, keepdims=True) / width
            weights = 1.0 / (1.0 + distance)
            scaled_ref[c : c + step, :width] = (weights * values).astype(BF16)
            scaled_ref[c : c + step, width:] = weight_columns(weights)
        member = member_ref[...]
        mass = tn(member, scaled_ref[:, width:])
        scale = 1.0 / (jnp.sum(mass, axis=1, keepdims=True) + 1.0)
        out_ref[...] = (tn(member, scaled_ref[:, :width]) + old_ref[...]) * scale
    out_copy = pltpu.make_async_copy(out_ref, out_hbm, sems.at[1])
    out_copy.start()
    rounded = out_ref[...].astype(BF16)
    slots = send_ref.shape[0]
    step = 256
    for s in range(0, slots, step):
        pick = onehot(iota((step, owned), 0) + s == slot_ref[...])
        send_ref[s : s + step, :] = nn(pick, rounded).astype(BF16)
    share_copy.wait()
    out_copy.wait()


def weight_columns(weights):
    n = weights.shape[0]
    hi = weights.astype(BF16).astype(F32)
    mid = (weights - hi).astype(BF16).astype(F32)
    low = weights - hi - mid
    lane = iota((n, 128), 1)
    cols = jnp.where(lane == 0, hi, jnp.where(lane == 1, mid, jnp.where(lane == 2, low, 0.0)))
    return cols.astype(BF16)


def member_two(group, got_ref, member_ref):
    total, share = member_ref.shape
    slots = got_ref.shape[0]
    devices = slots // group
    first = onehot(iota((devices, slots), 1) == iota((devices, slots), 0) * group)
    labels = nn(first, got_ref[:, got_ref.shape[1] - EXTRA :]).astype(BF16)
    expand = onehot(iota((total, devices), 0) // CAP_SHARE == iota((total, devices), 1))
    labels = nn(expand, labels)
    mine = iota((total, EXTRA), 1) == CAP_SHARE + iota((total, EXTRA), 0) % CAP_SHARE
    label = jnp.sum(jnp.where(mine, labels, 0.0), axis=1, keepdims=True).astype(jnp.int32) - 1
    member_ref[...] = onehot(iota((total, share), 1) == label)


def lloyd_two_kernel(got_ref, member_ref, centers_ref, out_ref, norm_ref, weighted_ref):
    share, width = centers_ref.shape
    total = got_ref.shape[0]
    step = 256
    centers = centers_ref[...]
    diagonal = iota((share, share), 0) == iota((share, share), 1)
    for t in range(ITER2):
        hi, lo = split2(centers)
        both = jnp.concatenate([hi, lo], axis=0)
        squares = jnp.sum(centers * centers, axis=1, keepdims=True)
        squares = jnp.sum(jnp.where(diagonal, squares, 0.0), axis=0, keepdims=True)
        for c in range(0, total, step):
            rows = got_ref[c : c + step, :]
            member = member_ref[c : c + step, :].astype(F32)
            if t == 0:
                values = rows.astype(F32)
                norm_ref[c : c + step, :] = jnp.sum(values * values, axis=1, keepdims=True)
            cross = nt(rows, both)
            cross = cross[:, :share] + cross[:, share:]
            rest = jnp.sum(member * (squares - 2.0 * cross), axis=1, keepdims=True)
            distance = jnp.maximum(norm_ref[c : c + step, :] + rest, 0.0) / width
            weights = member / (1.0 + distance)
            hi, lo = split2(weights)
            weighted_ref[c : c + step, :share] = hi
            weighted_ref[c : c + step, share:] = lo
        weighted = weighted_ref[...]
        sums = tn(weighted, got_ref[...])
        mass = tn(weighted, jnp.ones((total, 128), BF16))
        scale = 1.0 / (mass[:share, :1] + mass[share:, :1] + 1.0)
        centers = (sums[:share] + sums[share:] + centers) * scale
    out_ref[...] = centers.astype(BF16)


def place_kernel(places, groups, index_ref, *refs):
    blocks = refs[: len(places)]
    out_hbm, wide_ref, sems = refs[-3:]
    rows = blocks[0].shape[0]
    copies = []
    for i, (ref, (turn, flip)) in enumerate(zip(blocks, places)):
        wide_ref[i] = ref[...].astype(F32)
        held = lax.rem(index_ref[0] + groups - 2 * turn, groups)
        held = held + flip * (1 - 2 * lax.rem(held, 2))
        at = pl.multiple_of(held * rows, rows)
        copies.append(pltpu.make_async_copy(wide_ref.at[i], out_hbm.at[pl.ds(at, rows)], sems.at[i]))
        copies[-1].start()
    for copy in copies:
        copy.wait()


def whole():
    return pl.BlockSpec(memory_space=pltpu.VMEM)


def in_hbm():
    return pl.BlockSpec(memory_space=pltpu.HBM)


def keep_in_hbm(x):
    return pltpu.with_memory_space_constraint(x, pltpu.HBM)


def params(mib):
    return pltpu.CompilerParams(vmem_limit_bytes=mib * 1024 * 1024)


def pack_points(devices, subs, owned, share, assign, parent, points):
    iters = assign.shape[0]
    return pl.pallas_call(
        lambda *refs: pack_one_kernel(devices, owned, share, subs, *refs),
        out_shape=(
            jax.ShapeDtypeStruct((devices * CAP * iters, points.shape[1] + EXTRA), BF16),
            jax.ShapeDtypeStruct(parent.shape, jnp.int32),
        ),
        in_specs=[in_hbm()] * 3,
        out_specs=(whole(), whole()),
        scratch_shapes=[
            pltpu.VMEM(assign.shape, assign.dtype),
            pltpu.VMEM(parent.shape, parent.dtype),
            pltpu.VMEM(points.shape, points.dtype),
            pltpu.SemaphoreType.DMA((3,)),
        ],
        compiler_params=params(PACK_MIB),
        name="pack_points",
    )(keep_in_hbm(assign), keep_in_hbm(parent), keep_in_hbm(points))


def level_one(iters, devices, share, index, got, centers, slot_two, coarse):
    owned, width = centers.shape
    half = got.shape[0] // 2
    slots_two = devices * CAP_SHARE
    return pl.pallas_call(
        lambda *refs: lloyd_one_kernel(iters, *refs),
        out_shape=(
            pltpu.HBM((owned, width), F32),
            jax.ShapeDtypeStruct((slots_two, width), BF16),
            jax.ShapeDtypeStruct((slots_two, share), BF16),
            jax.ShapeDtypeStruct((share, width), F32),
        ),
        in_specs=[pl.BlockSpec(memory_space=pltpu.SMEM)] + [whole()] * 3 + [in_hbm()],
        out_specs=(in_hbm(), whole(), whole(), whole()),
        scratch_shapes=[
            pltpu.VMEM((owned, width), F32),
            pltpu.VMEM((half, width + EXTRA), BF16),
            pltpu.VMEM((half, owned), BF16),
            pltpu.SemaphoreType.DMA((2,)),
        ],
        compiler_params=params(ONE_MIB),
        name="level_one",
    )(index, got, centers, slot_two, keep_in_hbm(coarse))


def level_two(got, member, centers):
    slots, width = got.shape
    share = centers.shape[0]
    return pl.pallas_call(
        lloyd_two_kernel,
        out_shape=jax.ShapeDtypeStruct((share, width), BF16),
        in_specs=[whole()] * 3,
        out_specs=whole(),
        scratch_shapes=[
            pltpu.VMEM((slots, 1), F32),
            pltpu.VMEM((slots, 2 * share), BF16),
        ],
        compiler_params=params(TWO_MIB),
        name="level_two",
    )(got, member, centers)


def place(groups, index, blocks, out=None):
    places, arrays = list(blocks), list(blocks.values())
    share, width = arrays[0].shape
    extra = [] if out is None else [out]
    return pl.pallas_call(
        lambda *refs: place_kernel(places, groups, *refs),
        out_shape=pltpu.HBM((groups * share, width), F32),
        in_specs=[pl.BlockSpec(memory_space=pltpu.SMEM)] + [whole()] * len(arrays) + [in_hbm()] * len(extra),
        out_specs=in_hbm(),
        scratch_shapes=[pltpu.VMEM((len(arrays), share, width), F32), pltpu.SemaphoreType.DMA((len(arrays),))],
        input_output_aliases={1 + len(arrays): 0} if extra else {},
        compiler_params=params(PLACE_MIB),
        name="place_shares",
    )(index, *arrays, *extra)


def gather_shares(own, groups, index):
    blocks = {(0, 0): own}
    for k in TURNS:
        blocks[(k, 0)] = lax.ppermute(own, "grp", [(g, (g + 2 * k) % groups) for g in range(groups)])
    for k in (0, *TURNS):
        blocks[(k, 1)] = lax.ppermute(blocks[(k, 0)], "grp", [(g, g ^ 1) for g in range(groups)])
    last = TURNS[-1]
    out = place(groups, index, {p: b for p, b in blocks.items() if p[0] != last})
    return place(groups, index, {p: b for p, b in blocks.items() if p[0] == last}, out)


def shards(points, fine_initial, coarse_initial, assign, parent):
    groups = lax.axis_size("grp")
    subs = lax.axis_size("sub")
    devices = groups * subs
    iters = assign.shape[0]
    width = points.shape[1]
    owned = fine_initial.shape[0]
    share = coarse_initial.shape[0] // groups
    slots_two = devices * CAP_SHARE

    me = lax.axis_index("grp").astype(jnp.int32).reshape(1)
    send, slot_two = pack_points(devices, subs, owned, share, assign, parent.reshape(1, owned), points)
    send, me = lax.optimization_barrier((send, me))
    got = lax.all_to_all(
        send.reshape(devices, CAP * iters, width + EXTRA), ("grp", "sub"), split_axis=0, concat_axis=0, tiled=True
    ).reshape(devices * CAP * iters, width + EXTRA)
    fine, send_two, member, centers = level_one(
        iters, devices, share, me, got, fine_initial, slot_two, coarse_initial
    )
    got_two = lax.all_to_all(
        send_two.reshape(devices, CAP_SHARE, width), ("grp", "sub"), split_axis=0, concat_axis=0, tiled=True
    ).reshape(slots_two, width)
    own = level_two(got_two, member, centers)
    return fine, gather_shares(own, groups, me)


def solution(mesh):
    return jax.shard_map(
        shards,
        mesh=mesh,
        in_specs=(
            P(("grp", "sub"), None),
            P(("grp", "sub"), None),
            P("sub", None),
            P(None, ("grp", "sub")),
            P(("grp", "sub")),
        ),
        out_specs=(P(("grp", "sub"), None), P("sub", None)),
        check_vma=False,
    )
```

```python
import jax
import jax.numpy as jnp
from jax import lax
from jax.experimental import pallas as pl
from jax.experimental.pallas import tpu as pltpu
from jax.sharding import PartitionSpec as P

ITER2 = 2
CAP = 4
CAP_SHARE = 16
EXTRA = 128
DIGIT = 32
F32 = jnp.float32
BF16 = jnp.bfloat16
GATHER_STEP = 128
PACK_STEP = 256
TWO_STEP = 256
TURNS = (2, 1, 3)
PACK_MIB = 16
ONE_MIB = 36
TWO_MIB = 24
PLACE_MIB = 16


def nt(a, b):
    return lax.dot_general(a, b, (((1,), (1,)), ((), ())), preferred_element_type=F32)


def tn(a, b):
    return lax.dot_general(a, b, (((0,), (0,)), ((), ())), preferred_element_type=F32)


def nn(a, b):
    return lax.dot_general(a, b, (((1,), (0,)), ((), ())), preferred_element_type=F32)


def iota(shape, dim):
    return lax.broadcasted_iota(jnp.int32, shape, dim)


def onehot(mask):
    return jnp.where(mask, 1.0, 0.0).astype(BF16)


def split2(x):
    hi = x.astype(BF16)
    lo = (x - hi.astype(F32)).astype(BF16)
    return hi, lo


def rank_in_bucket(member):
    n = member.shape[1]
    step = 128
    ones = jnp.where(member, 1.0, 0.0)
    earlier = onehot(iota((step, step), 0) < iota((step, step), 1))
    seen = jnp.zeros((member.shape[0], 1), F32)
    ranks = []
    for c in range(0, n, step):
        block = ones[:, c : c + step]
        before = nn(block.astype(BF16), earlier) + seen
        ranks.append(jnp.sum(block * before, axis=0, keepdims=True))
        seen = seen + jnp.sum(block, axis=1, keepdims=True)
    return jnp.concatenate(ranks, axis=1).astype(jnp.int32)


def pack_one_kernel(
    devices, owned, share, subs, assign_hbm, parent_hbm, points_hbm, out_ref, slot_ref, assign_ref, parent_ref, points_ref, sems
):
    copies = [
        pltpu.make_async_copy(parent_hbm, parent_ref, sems.at[0]),
        pltpu.make_async_copy(assign_hbm, assign_ref, sems.at[1]),
        pltpu.make_async_copy(points_hbm, points_ref, sems.at[2]),
    ]
    for copy in copies:
        copy.start()
    copies[0].wait()
    iters, n = assign_ref.shape
    group = CAP * iters
    slots = devices * group
    width = points_ref.shape[1]

    parent = parent_ref[...]
    k = parent.shape[1]
    per_sub = share * (devices // subs)
    dest = (parent % per_sub) // share * subs + parent // per_sub
    member = iota((devices, k), 0) == dest
    rank = rank_in_bucket(member)
    slot_ref[...] = dest * CAP_SHARE + rank
    lane = iota((EXTRA, k), 0)
    labels = jnp.where(lane == CAP_SHARE + rank, parent % share + 1, 0)
    labels = nt(onehot(member), labels.astype(F32).astype(BF16)).astype(BF16)
    spread = onehot(iota((slots, devices), 0) == iota((slots, devices), 1) * group)
    extra = nn(spread, labels)

    copies[1].wait()
    hot = None
    slot_iota = iota((slots, n), 0)
    for t in range(iters):
        target = assign_ref[t : t + 1, :]
        dest = target // owned
        local = target % owned
        rank = rank_in_bucket(iota((devices, n), 0) == dest)
        mask = slot_iota == dest * group + t * CAP + rank
        hot = mask if hot is None else jnp.logical_or(hot, mask)
        lane = iota((EXTRA, n), 0)
        digits = jnp.where(lane == 0, local // DIGIT + 1, jnp.where(lane == 1, local % DIGIT, 0))
        extra = extra + nt(onehot(mask), digits.astype(F32).astype(BF16))
    out_ref[:, width:] = extra.astype(BF16)
    copies[2].wait()
    out_ref[:, :width] = nn(onehot(hot), points_ref[...]).astype(BF16)


def lloyd_one_kernel(
    iters, index_ref, got_ref, centers_ref, slot_ref, coarse_hbm, out_ref, send_ref, two_ref, share_ref, scaled_ref, member_ref, sem
):
    share = share_ref.shape[0]
    start = pl.multiple_of(index_ref[0] * share, share)
    share_copy = pltpu.make_async_copy(coarse_hbm.at[pl.ds(start, share)], share_ref, sem)
    share_copy.start()
    owned, width = centers_ref.shape
    group = CAP * iters
    total = got_ref.shape[0]
    half = total // 2
    step = GATHER_STEP
    low = iota((step, EXTRA), 0) % 8 < CAP
    wide_low = iota((step, width), 0) % 8 < CAP
    for t in range(iters):
        old_ref = centers_ref if t == 0 else out_ref
        rounded = old_ref[...].astype(BF16)
        mass = jnp.zeros((1, owned), F32)
        for c in range(0, half, step):
            def rows(lo, hi, keep):
                got = got_ref[2 * c : 2 * (c + step), lo:hi].astype(F32).reshape(step // 8, 16, hi - lo)
                even = got[:, 0:8, :].reshape(step, hi - lo)
                odd = got[:, 8:16, :].reshape(step, hi - lo)
                if t == 0:
                    return jnp.where(keep, even, pltpu.roll(odd, CAP, 0))
                return jnp.where(keep, pltpu.roll(even, step - CAP, 0), odd)

            extra = rows(width, width + EXTRA, low)
            values = rows(0, width, wide_low)
            label = ((extra[:, 0:1] - 1.0) * DIGIT + extra[:, 1:2]).astype(jnp.int32)
            mask = iota((step, owned), 1) == label
            member = onehot(mask)
            member_ref[c : c + step, :] = member
            nearest = nn(member, rounded)
            distance = jnp.sum((values - nearest) ** 2, axis=1, keepdims=True) / width
            weights = 1.0 / (1.0 + distance)
            scaled_ref[c : c + step, :] = (weights * values).astype(BF16)
            mass = mass + jnp.sum(jnp.where(mask, weights, 0.0), axis=0, keepdims=True)
        scale = 1.0 / (as_column(mass) + 1.0)
        out_ref[...] = (tn(member_ref[...], scaled_ref[...]) + old_ref[...]) * scale
    rounded = out_ref[...].astype(BF16)
    slots = send_ref.shape[0]
    step = PACK_STEP
    for s in range(0, slots, step):
        pick = onehot(iota((step, owned), 0) + s == slot_ref[...])
        send_ref[s : s + step, :] = nn(pick, rounded).astype(BF16)
    member_two(group, got_ref, two_ref)
    share_copy.wait()


def as_column(row):
    step = 128
    diagonal = iota((step, step), 0) == iota((step, step), 1)
    parts = [
        jnp.sum(jnp.where(diagonal, row[:, c : c + step], 0.0), axis=1, keepdims=True) for c in range(0, row.shape[1], step)
    ]
    return jnp.concatenate(parts, axis=0)


def member_two(group, got_ref, member_ref):
    total, share = member_ref.shape
    slots = got_ref.shape[0]
    devices = slots // group
    first = onehot(iota((devices, slots), 1) == iota((devices, slots), 0) * group)
    labels = nn(first, got_ref[:, got_ref.shape[1] - EXTRA :]).astype(BF16)
    expand = onehot(iota((total, devices), 0) // CAP_SHARE == iota((total, devices), 1))
    labels = nn(expand, labels)
    mine = iota((total, EXTRA), 1) == CAP_SHARE + iota((total, EXTRA), 0) % CAP_SHARE
    label = jnp.sum(jnp.where(mine, labels, 0.0), axis=1, keepdims=True).astype(jnp.int32) - 1
    member_ref[...] = onehot(iota((total, share), 1) == label)


def lloyd_two_kernel(got_ref, member_ref, centers_ref, out_ref, norm_ref, weighted_ref):
    share, width = centers_ref.shape
    total = got_ref.shape[0]
    step = TWO_STEP
    centers = centers_ref[...]
    diagonal = iota((share, share), 0) == iota((share, share), 1)
    for t in range(ITER2):
        hi, lo = split2(centers)
        both = jnp.concatenate([hi, lo], axis=0)
        squares = jnp.sum(centers * centers, axis=1, keepdims=True)
        squares = jnp.sum(jnp.where(diagonal, squares, 0.0), axis=0, keepdims=True)
        mass = jnp.zeros((1, share), F32)
        for c in range(0, total, step):
            rows = got_ref[c : c + step, :]
            member = member_ref[c : c + step, :].astype(F32)
            if t == 0:
                values = rows.astype(F32)
                norm_ref[c : c + step, :] = jnp.sum(values * values, axis=1, keepdims=True)
            cross = nt(rows, both)
            cross = cross[:, :share] + cross[:, share:]
            rest = jnp.sum(member * (squares - 2.0 * cross), axis=1, keepdims=True)
            distance = jnp.maximum(norm_ref[c : c + step, :] + rest, 0.0) / width
            weights = member / (1.0 + distance)
            mass = mass + jnp.sum(weights, axis=0, keepdims=True)
            hi, lo = split2(weights)
            weighted_ref[c : c + step, :share] = hi
            weighted_ref[c : c + step, share:] = lo
        sums = tn(weighted_ref[...], got_ref[...])
        scale = 1.0 / (as_column(mass) + 1.0)
        centers = (sums[:share] + sums[share:] + centers) * scale
    out_ref[...] = centers.astype(BF16)


def place_kernel(places, groups, index_ref, *refs):
    blocks = refs[: len(places)]
    out_hbm, wide_ref, sems = refs[-3:]
    rows = blocks[0].shape[0]
    copies = []
    for i, (ref, (turn, flip)) in enumerate(zip(blocks, places)):
        wide_ref[i] = ref[...].astype(F32)
        held = lax.rem(index_ref[0] + groups - 2 * turn, groups)
        held = held + flip * (1 - 2 * lax.rem(held, 2))
        at = pl.multiple_of(held * rows, rows)
        copies.append(pltpu.make_async_copy(wide_ref.at[i], out_hbm.at[pl.ds(at, rows)], sems.at[i]))
        copies[-1].start()
    for copy in copies:
        copy.wait()


def place_first_kernel(places, groups, index_ref, fine_ref, *refs):
    fine_hbm, fine_sem = refs[len(places)], refs[-1]
    fine_copy = pltpu.make_async_copy(fine_ref, fine_hbm, fine_sem)
    fine_copy.start()
    place_kernel(places, groups, index_ref, *refs[: len(places)], *refs[len(places) + 1 : -1])
    fine_copy.wait()


def whole():
    return pl.BlockSpec(memory_space=pltpu.VMEM)


def in_hbm():
    return pl.BlockSpec(memory_space=pltpu.HBM)


def keep_in_hbm(x):
    return pltpu.with_memory_space_constraint(x, pltpu.HBM)


def params(mib):
    return pltpu.CompilerParams(vmem_limit_bytes=mib * 1024 * 1024)


def pack_points(devices, subs, owned, share, assign, parent, points):
    iters = assign.shape[0]
    return pl.pallas_call(
        lambda *refs: pack_one_kernel(devices, owned, share, subs, *refs),
        out_shape=(
            jax.ShapeDtypeStruct((devices * CAP * iters, points.shape[1] + EXTRA), BF16),
            jax.ShapeDtypeStruct(parent.shape, jnp.int32),
        ),
        in_specs=[in_hbm()] * 3,
        out_specs=(whole(), whole()),
        scratch_shapes=[
            pltpu.VMEM(assign.shape, assign.dtype),
            pltpu.VMEM(parent.shape, parent.dtype),
            pltpu.VMEM(points.shape, points.dtype),
            pltpu.SemaphoreType.DMA((3,)),
        ],
        compiler_params=params(PACK_MIB),
        name="pack_points",
    )(keep_in_hbm(assign), keep_in_hbm(parent), keep_in_hbm(points))


def level_one(iters, devices, share, index, got, centers, slot_two, coarse):
    owned, width = centers.shape
    half = got.shape[0] // 2
    slots_two = devices * CAP_SHARE
    return pl.pallas_call(
        lambda *refs: lloyd_one_kernel(iters, *refs),
        out_shape=(
            pltpu.VMEM((owned, width), F32),
            jax.ShapeDtypeStruct((slots_two, width), BF16),
            jax.ShapeDtypeStruct((slots_two, share), BF16),
            jax.ShapeDtypeStruct((share, width), F32),
        ),
        in_specs=[pl.BlockSpec(memory_space=pltpu.SMEM)] + [whole()] * 3 + [in_hbm()],
        out_specs=(whole(),) * 4,
        scratch_shapes=[
            pltpu.VMEM((half, width), BF16),
            pltpu.VMEM((half, owned), BF16),
            pltpu.SemaphoreType.DMA,
        ],
        compiler_params=params(ONE_MIB),
        name="level_one",
    )(index, got, centers, slot_two, keep_in_hbm(coarse))


def level_two(got, member, centers):
    slots, width = got.shape
    share = centers.shape[0]
    return pl.pallas_call(
        lloyd_two_kernel,
        out_shape=jax.ShapeDtypeStruct((share, width), BF16),
        in_specs=[whole()] * 3,
        out_specs=whole(),
        scratch_shapes=[
            pltpu.VMEM((slots, 1), F32),
            pltpu.VMEM((slots, 2 * share), BF16),
        ],
        compiler_params=params(TWO_MIB),
        name="level_two",
    )(got, member, centers)


def place(groups, index, blocks, out=None, fine=None):
    places, arrays = list(blocks), list(blocks.values())
    share, width = arrays[0].shape
    kernel, before, after = place_kernel, [], [out]
    out_shape, out_specs = pltpu.HBM((groups * share, width), F32), in_hbm()
    scratch = [pltpu.VMEM((len(arrays), share, width), F32), pltpu.SemaphoreType.DMA((len(arrays),))]
    if out is None:
        kernel, before, after = place_first_kernel, [fine], []
        out_shape, out_specs = (pltpu.HBM(fine.shape, F32), out_shape), (in_hbm(), in_hbm())
        scratch.append(pltpu.SemaphoreType.DMA)
    return pl.pallas_call(
        lambda *refs: kernel(places, groups, *refs),
        out_shape=out_shape,
        in_specs=[pl.BlockSpec(memory_space=pltpu.SMEM)]
        + [whole()] * (len(before) + len(arrays))
        + [in_hbm()] * len(after),
        out_specs=out_specs,
        scratch_shapes=scratch,
        input_output_aliases={1 + len(arrays): 0} if after else {},
        compiler_params=params(PLACE_MIB),
        cost_estimate=pl.CostEstimate(
            flops=len(arrays) * share * width, bytes_accessed=len(arrays) * share * width * 6, transcendentals=0
        ),
        name="place_shares",
    )(index, *before, *arrays, *after)


def gather_shares(own, groups, index, fine):
    def other_core(rows):
        return lax.ppermute(rows, "grp", [(g, g ^ 1) for g in range(groups)])

    far = [lax.ppermute(own, "grp", [(g, (g + 2 * k) % groups) for g in range(groups)]) for k in TURNS]
    fine, out = place(groups, index, {(0, 0): own}, fine=fine)
    out, own = lax.optimization_barrier((out, own))
    blocks = {(0, 1): other_core(own)}
    for k, rows in zip(TURNS, far):
        out, rows = lax.optimization_barrier((out, rows))
        blocks |= {(k, 0): rows, (k, 1): other_core(rows)}
    return fine, place(groups, index, blocks, out)


def shards(points, fine_initial, coarse_initial, assign, parent):
    groups = lax.axis_size("grp")
    subs = lax.axis_size("sub")
    devices = groups * subs
    iters = assign.shape[0]
    width = points.shape[1]
    owned = fine_initial.shape[0]
    share = coarse_initial.shape[0] // groups
    slots_two = devices * CAP_SHARE

    me = lax.axis_index("grp").astype(jnp.int32).reshape(1)
    send, slot_two = pack_points(devices, subs, owned, share, assign, parent.reshape(1, owned), points)
    send, me = lax.optimization_barrier((send, me))
    got = lax.all_to_all(
        send.reshape(devices, CAP * iters, width + EXTRA), ("grp", "sub"), split_axis=0, concat_axis=0, tiled=True
    ).reshape(devices * CAP * iters, width + EXTRA)
    fine, send_two, member, centers = level_one(
        iters, devices, share, me, got, fine_initial, slot_two, coarse_initial
    )
    got_two = lax.all_to_all(
        send_two.reshape(devices, CAP_SHARE, width), ("grp", "sub"), split_axis=0, concat_axis=0, tiled=True
    ).reshape(slots_two, width)
    own = level_two(got_two, member, centers)
    return gather_shares(own, groups, me, fine)


def solution(mesh):
    return jax.shard_map(
        shards,
        mesh=mesh,
        in_specs=(
            P(("grp", "sub"), None),
            P(("grp", "sub"), None),
            P("sub", None),
            P(None, ("grp", "sub")),
            P(("grp", "sub")),
        ),
        out_specs=(P(("grp", "sub"), None), P("sub", None)),
        check_vma=False,
    )
```

```python
import jax
import jax.numpy as jnp
from jax import lax
from jax.experimental import pallas as pl
from jax.experimental.pallas import tpu as pltpu
from jax.sharding import PartitionSpec as P

ITER2 = 2
CAP = 4
CAP_SHARE = 16
EXTRA = 128
DIGIT = 32
F32 = jnp.float32
BF16 = jnp.bfloat16
GATHER_STEP = 128
PACK_STEP = 256
TWO_STEP = 256
TURNS = (2, 1, 3)
PACK_MIB = 16
ONE_MIB = 36
TWO_MIB = 24
PLACE_MIB = 16


def nt(a, b):
    return lax.dot_general(a, b, (((1,), (1,)), ((), ())), preferred_element_type=F32)


def tn(a, b):
    return lax.dot_general(a, b, (((0,), (0,)), ((), ())), preferred_element_type=F32)


def nn(a, b):
    return lax.dot_general(a, b, (((1,), (0,)), ((), ())), preferred_element_type=F32)


def iota(shape, dim):
    return lax.broadcasted_iota(jnp.int32, shape, dim)


def onehot(mask):
    return jnp.where(mask, 1.0, 0.0).astype(BF16)


def split2(x):
    hi = x.astype(BF16)
    lo = (x - hi.astype(F32)).astype(BF16)
    return hi, lo


def rank_in_bucket(member):
    n = member.shape[1]
    step = 128
    ones = jnp.where(member, 1.0, 0.0)
    earlier = onehot(iota((step, step), 0) < iota((step, step), 1))
    seen = jnp.zeros((member.shape[0], 1), F32)
    ranks = []
    for c in range(0, n, step):
        block = ones[:, c : c + step]
        before = nn(block.astype(BF16), earlier) + seen
        ranks.append(jnp.sum(block * before, axis=0, keepdims=True))
        seen = seen + jnp.sum(block, axis=1, keepdims=True)
    return jnp.concatenate(ranks, axis=1).astype(jnp.int32)


def pack_one_kernel(
    devices, owned, share, subs, assign_hbm, parent_hbm, points_hbm, out_ref, slot_ref, assign_ref, parent_ref, points_ref, sems
):
    copies = [
        pltpu.make_async_copy(parent_hbm, parent_ref, sems.at[0]),
        pltpu.make_async_copy(assign_hbm, assign_ref, sems.at[1]),
        pltpu.make_async_copy(points_hbm, points_ref, sems.at[2]),
    ]
    for copy in copies:
        copy.start()
    iters, n = assign_ref.shape
    slots = devices * CAP
    width = points_ref.shape[1]

    spread = onehot(iota((slots, devices), 0) == iota((slots, devices), 1) * CAP)
    copies[0].wait()
    parent = parent_ref[...]
    k = parent.shape[1]
    per_sub = share * (devices // subs)
    dest = (parent % per_sub) // share * subs + parent // per_sub
    member = iota((devices, k), 0) == dest
    rank = rank_in_bucket(member)
    slot_ref[...] = dest * CAP_SHARE + rank
    lane = iota((EXTRA, k), 0)
    labels = jnp.where(lane == CAP_SHARE + rank, parent % share + 1, 0)
    labels = nt(onehot(member), labels.astype(F32).astype(BF16)).astype(BF16)
    extra = nn(spread, labels)

    copies[1].wait()
    slot_iota = iota((slots, n), 0)
    for t in range(iters):
        target = assign_ref[t : t + 1, :]
        dest = target // owned
        local = target % owned
        rank = rank_in_bucket(iota((devices, n), 0) == dest)
        hot = onehot(slot_iota == dest * CAP + rank)
        lane = iota((EXTRA, n), 0) - 2 * t
        digits = jnp.where(lane == 0, local // DIGIT + 1, jnp.where(lane == 1, local % DIGIT, 0))
        extra = extra + nt(hot, digits.astype(F32).astype(BF16))
        if t == 0:
            copies[2].wait()
        rows = nn(hot, points_ref[...]).reshape(devices, CAP, width)
        out_ref[:, :, t * width : (t + 1) * width] = rows.astype(BF16)
    out_ref[:, :, iters * width :] = extra.reshape(devices, CAP, EXTRA).astype(BF16)


def lloyd_one_kernel(
    iters, index_ref, got_ref, centers_ref, slot_ref, coarse_hbm, out_ref, send_ref, two_ref, share_ref, scaled_ref, member_ref, sem
):
    share = share_ref.shape[0]
    start = pl.multiple_of(index_ref[0] * share, share)
    share_copy = pltpu.make_async_copy(coarse_hbm.at[pl.ds(start, share)], share_ref, sem)
    share_copy.start()
    owned, width = centers_ref.shape
    half = got_ref.shape[0] * CAP
    step = GATHER_STEP
    for t in range(iters):
        old_ref = centers_ref if t == 0 else out_ref
        rounded = old_ref[...].astype(BF16)
        mass = jnp.zeros((1, owned), F32)
        for c in range(0, half, step):
            def rows(lo, size):
                got = got_ref[c // CAP : (c + step) // CAP, :, lo : lo + size]
                return got.astype(F32).reshape(step, size)

            extra = rows(iters * width, EXTRA)
            values = rows(t * width, width)
            label = ((extra[:, 2 * t : 2 * t + 1] - 1.0) * DIGIT + extra[:, 2 * t + 1 : 2 * t + 2]).astype(jnp.int32)
            mask = iota((step, owned), 1) == label
            member = onehot(mask)
            member_ref[c : c + step, :] = member
            nearest = nn(member, rounded)
            distance = jnp.sum((values - nearest) ** 2, axis=1, keepdims=True) / width
            weights = 1.0 / (1.0 + distance)
            scaled_ref[c : c + step, :] = (weights * values).astype(BF16)
            mass = mass + jnp.sum(jnp.where(mask, weights, 0.0), axis=0, keepdims=True)
        scale = 1.0 / (as_column(mass) + 1.0)
        out_ref[...] = (tn(member_ref[...], scaled_ref[...]) + old_ref[...]) * scale
    rounded = out_ref[...].astype(BF16)
    slots = send_ref.shape[0]
    step = PACK_STEP
    for s in range(0, slots, step):
        pick = onehot(iota((step, owned), 0) + s == slot_ref[...])
        send_ref[s : s + step, :] = nn(pick, rounded).astype(BF16)
    member_two(got_ref, two_ref)
    share_copy.wait()


def as_column(row):
    step = 128
    diagonal = iota((step, step), 0) == iota((step, step), 1)
    parts = [
        jnp.sum(jnp.where(diagonal, row[:, c : c + step], 0.0), axis=1, keepdims=True) for c in range(0, row.shape[1], step)
    ]
    return jnp.concatenate(parts, axis=0)


def member_two(got_ref, member_ref):
    total, share = member_ref.shape
    devices = got_ref.shape[0]
    slots = devices * CAP
    first = onehot(iota((devices, slots), 1) == iota((devices, slots), 0) * CAP)
    extra = got_ref[:, :, got_ref.shape[2] - EXTRA :].astype(F32).reshape(slots, EXTRA)
    labels = nn(first, extra.astype(BF16)).astype(BF16)
    expand = onehot(iota((total, devices), 0) // CAP_SHARE == iota((total, devices), 1))
    labels = nn(expand, labels)
    mine = iota((total, EXTRA), 1) == CAP_SHARE + iota((total, EXTRA), 0) % CAP_SHARE
    label = jnp.sum(jnp.where(mine, labels, 0.0), axis=1, keepdims=True).astype(jnp.int32) - 1
    member_ref[...] = onehot(iota((total, share), 1) == label)


def lloyd_two_kernel(got_ref, member_ref, centers_ref, out_ref, norm_ref, weighted_ref):
    share, width = centers_ref.shape
    total = got_ref.shape[0]
    step = TWO_STEP
    centers = centers_ref[...]
    diagonal = iota((share, share), 0) == iota((share, share), 1)
    for t in range(ITER2):
        hi, lo = split2(centers)
        both = jnp.concatenate([hi, lo], axis=0)
        squares = jnp.sum(centers * centers, axis=1, keepdims=True)
        squares = jnp.sum(jnp.where(diagonal, squares, 0.0), axis=0, keepdims=True)
        mass = jnp.zeros((1, share), F32)
        for c in range(0, total, step):
            rows = got_ref[c : c + step, :]
            member = member_ref[c : c + step, :].astype(F32)
            if t == 0:
                values = rows.astype(F32)
                norm_ref[c : c + step, :] = jnp.sum(values * values, axis=1, keepdims=True)
            cross = nt(rows, both)
            cross = cross[:, :share] + cross[:, share:]
            rest = jnp.sum(member * (squares - 2.0 * cross), axis=1, keepdims=True)
            distance = jnp.maximum(norm_ref[c : c + step, :] + rest, 0.0) / width
            weights = member / (1.0 + distance)
            mass = mass + jnp.sum(weights, axis=0, keepdims=True)
            hi, lo = split2(weights)
            weighted_ref[c : c + step, :share] = hi
            weighted_ref[c : c + step, share:] = lo
        sums = tn(weighted_ref[...], got_ref[...])
        scale = 1.0 / (as_column(mass) + 1.0)
        centers = (sums[:share] + sums[share:] + centers) * scale
    out_ref[...] = centers.astype(BF16)


def place_kernel(places, groups, index_ref, *refs):
    blocks = refs[: len(places)]
    out_hbm, wide_ref, sems = refs[-3:]
    rows = blocks[0].shape[0]
    copies = []
    for i, (ref, (turn, flip)) in enumerate(zip(blocks, places)):
        wide_ref[i] = ref[...].astype(F32)
        held = lax.rem(index_ref[0] + groups - 2 * turn, groups)
        held = held + flip * (1 - 2 * lax.rem(held, 2))
        at = pl.multiple_of(held * rows, rows)
        copies.append(pltpu.make_async_copy(wide_ref.at[i], out_hbm.at[pl.ds(at, rows)], sems.at[i]))
        copies[-1].start()
    for copy in copies:
        copy.wait()


def place_first_kernel(places, groups, index_ref, fine_ref, *refs):
    fine_hbm, fine_sem = refs[len(places)], refs[-1]
    fine_copy = pltpu.make_async_copy(fine_ref, fine_hbm, fine_sem)
    fine_copy.start()
    place_kernel(places, groups, index_ref, *refs[: len(places)], *refs[len(places) + 1 : -1])
    fine_copy.wait()


def whole():
    return pl.BlockSpec(memory_space=pltpu.VMEM)


def in_hbm():
    return pl.BlockSpec(memory_space=pltpu.HBM)


def keep_in_hbm(x):
    return pltpu.with_memory_space_constraint(x, pltpu.HBM)


def params(mib):
    return pltpu.CompilerParams(vmem_limit_bytes=mib * 1024 * 1024)


def pack_points(devices, subs, owned, share, assign, parent, points):
    iters = assign.shape[0]
    return pl.pallas_call(
        lambda *refs: pack_one_kernel(devices, owned, share, subs, *refs),
        out_shape=(
            jax.ShapeDtypeStruct((devices, CAP, iters * points.shape[1] + EXTRA), BF16),
            jax.ShapeDtypeStruct(parent.shape, jnp.int32),
        ),
        in_specs=[in_hbm()] * 3,
        out_specs=(whole(), whole()),
        scratch_shapes=[
            pltpu.VMEM(assign.shape, assign.dtype),
            pltpu.VMEM(parent.shape, parent.dtype),
            pltpu.VMEM(points.shape, points.dtype),
            pltpu.SemaphoreType.DMA((3,)),
        ],
        compiler_params=params(PACK_MIB),
        name="pack_points",
    )(keep_in_hbm(assign), keep_in_hbm(parent), keep_in_hbm(points))


def level_one(iters, devices, share, index, got, centers, slot_two, coarse):
    owned, width = centers.shape
    half = devices * CAP
    slots_two = devices * CAP_SHARE
    return pl.pallas_call(
        lambda *refs: lloyd_one_kernel(iters, *refs),
        out_shape=(
            pltpu.VMEM((owned, width), F32),
            jax.ShapeDtypeStruct((slots_two, width), BF16),
            jax.ShapeDtypeStruct((slots_two, share), BF16),
            jax.ShapeDtypeStruct((share, width), F32),
        ),
        in_specs=[pl.BlockSpec(memory_space=pltpu.SMEM)] + [whole()] * 3 + [in_hbm()],
        out_specs=(whole(),) * 4,
        scratch_shapes=[
            pltpu.VMEM((half, width), BF16),
            pltpu.VMEM((half, owned), BF16),
            pltpu.SemaphoreType.DMA,
        ],
        compiler_params=params(ONE_MIB),
        name="level_one",
    )(index, got, centers, slot_two, keep_in_hbm(coarse))


def level_two(got, member, centers):
    slots, width = got.shape
    share = centers.shape[0]
    return pl.pallas_call(
        lloyd_two_kernel,
        out_shape=jax.ShapeDtypeStruct((share, width), BF16),
        in_specs=[whole()] * 3,
        out_specs=whole(),
        scratch_shapes=[
            pltpu.VMEM((slots, 1), F32),
            pltpu.VMEM((slots, 2 * share), BF16),
        ],
        compiler_params=params(TWO_MIB),
        name="level_two",
    )(got, member, centers)


def place(groups, index, blocks, out=None, fine=None):
    places, arrays = list(blocks), list(blocks.values())
    share, width = arrays[0].shape
    kernel, before, after = place_kernel, [], [out]
    out_shape, out_specs = pltpu.HBM((groups * share, width), F32), in_hbm()
    scratch = [pltpu.VMEM((len(arrays), share, width), F32), pltpu.SemaphoreType.DMA((len(arrays),))]
    if out is None:
        kernel, before, after = place_first_kernel, [fine], []
        out_shape, out_specs = (pltpu.HBM(fine.shape, F32), out_shape), (in_hbm(), in_hbm())
        scratch.append(pltpu.SemaphoreType.DMA)
    return pl.pallas_call(
        lambda *refs: kernel(places, groups, *refs),
        out_shape=out_shape,
        in_specs=[pl.BlockSpec(memory_space=pltpu.SMEM)]
        + [whole()] * (len(before) + len(arrays))
        + [in_hbm()] * len(after),
        out_specs=out_specs,
        scratch_shapes=scratch,
        input_output_aliases={1 + len(arrays): 0} if after else {},
        compiler_params=params(PLACE_MIB),
        cost_estimate=pl.CostEstimate(
            flops=len(arrays) * share * width, bytes_accessed=len(arrays) * share * width * 6, transcendentals=0
        ),
        name="place_shares",
    )(index, *before, *arrays, *after)


def gather_shares(own, groups, index, fine):
    def other_core(rows):
        return lax.ppermute(rows, "grp", [(g, g ^ 1) for g in range(groups)])

    far = [lax.ppermute(own, "grp", [(g, (g + 2 * k) % groups) for g in range(groups)]) for k in TURNS]
    fine, out = place(groups, index, {(0, 0): own}, fine=fine)
    out, own = lax.optimization_barrier((out, own))
    blocks = {(0, 1): other_core(own)}
    for k, rows in zip(TURNS, far):
        out, rows = lax.optimization_barrier((out, rows))
        blocks |= {(k, 0): rows, (k, 1): other_core(rows)}
    return fine, place(groups, index, blocks, out)


def shards(points, fine_initial, coarse_initial, assign, parent):
    groups = lax.axis_size("grp")
    subs = lax.axis_size("sub")
    devices = groups * subs
    iters = assign.shape[0]
    width = points.shape[1]
    owned = fine_initial.shape[0]
    share = coarse_initial.shape[0] // groups
    slots_two = devices * CAP_SHARE

    me = lax.axis_index("grp").astype(jnp.int32).reshape(1)
    send, slot_two = pack_points(devices, subs, owned, share, assign, parent.reshape(1, owned), points)
    send, me = lax.optimization_barrier((send, me))
    got = lax.all_to_all(send, ("grp", "sub"), split_axis=0, concat_axis=0, tiled=True)
    fine, send_two, member, centers = level_one(
        iters, devices, share, me, got, fine_initial, slot_two, coarse_initial
    )
    got_two = lax.all_to_all(
        send_two.reshape(devices, CAP_SHARE, width), ("grp", "sub"), split_axis=0, concat_axis=0, tiled=True
    ).reshape(slots_two, width)
    own = level_two(got_two, member, centers)
    return gather_shares(own, groups, me, fine)


def solution(mesh):
    return jax.shard_map(
        shards,
        mesh=mesh,
        in_specs=(
            P(("grp", "sub"), None),
            P(("grp", "sub"), None),
            P("sub", None),
            P(None, ("grp", "sub")),
            P(("grp", "sub")),
        ),
        out_specs=(P(("grp", "sub"), None), P("sub", None)),
        check_vma=False,
    )
```

```python
import jax
import jax.numpy as jnp
from jax import lax
from jax.experimental import pallas as pl
from jax.experimental.pallas import tpu as pltpu
from jax.sharding import PartitionSpec as P

ITER2 = 2
CAP = 4
ROWS = 2
CAP_SHARE = 16
EXTRA = 128
DIGIT = 32
F32 = jnp.float32
BF16 = jnp.bfloat16
GATHER_STEP = 128
PACK_STEP = 256
TWO_STEP = 256
TURNS = (2, 1, 3)
PACK_MIB = 16
ONE_MIB = 36
TWO_MIB = 24
PLACE_MIB = 16


def nt(a, b):
    return lax.dot_general(a, b, (((1,), (1,)), ((), ())), preferred_element_type=F32)


def tn(a, b):
    return lax.dot_general(a, b, (((0,), (0,)), ((), ())), preferred_element_type=F32)


def nn(a, b):
    return lax.dot_general(a, b, (((1,), (0,)), ((), ())), preferred_element_type=F32)


def iota(shape, dim):
    return lax.broadcasted_iota(jnp.int32, shape, dim)


def onehot(mask):
    return jnp.where(mask, 1.0, 0.0).astype(BF16)


def split2(x):
    hi = x.astype(BF16)
    lo = (x - hi.astype(F32)).astype(BF16)
    return hi, lo


def rank_in_bucket(member):
    n = member.shape[1]
    step = 128
    ones = jnp.where(member, 1.0, 0.0)
    earlier = onehot(iota((step, step), 0) < iota((step, step), 1))
    seen = jnp.zeros((member.shape[0], 1), F32)
    ranks = []
    for c in range(0, n, step):
        block = ones[:, c : c + step]
        before = nn(block.astype(BF16), earlier) + seen
        ranks.append(jnp.sum(block * before, axis=0, keepdims=True))
        seen = seen + jnp.sum(block, axis=1, keepdims=True)
    return jnp.concatenate(ranks, axis=1).astype(jnp.int32)


def pack_one_kernel(
    devices, owned, share, subs, assign_hbm, parent_hbm, points_hbm, out_ref, slot_ref, assign_ref, parent_ref, points_ref, sems
):
    copies = [
        pltpu.make_async_copy(parent_hbm, parent_ref, sems.at[0]),
        pltpu.make_async_copy(assign_hbm, assign_ref, sems.at[1]),
        pltpu.make_async_copy(points_hbm, points_ref, sems.at[2]),
    ]
    for copy in copies:
        copy.start()
    iters, n = assign_ref.shape
    slots = devices * ROWS
    width = points_ref.shape[1]

    spread = onehot(iota((slots, devices), 0) == iota((slots, devices), 1) * ROWS)
    copies[0].wait()
    parent = parent_ref[...]
    k = parent.shape[1]
    per_sub = share * (devices // subs)
    dest = (parent % per_sub) // share * subs + parent // per_sub
    member = iota((devices, k), 0) == dest
    rank = rank_in_bucket(member)
    slot_ref[...] = dest * CAP_SHARE + rank
    lane = iota((EXTRA, k), 0)
    labels = jnp.where(lane == CAP_SHARE + rank, parent % share + 1, 0)
    labels = nt(onehot(member), labels.astype(F32).astype(BF16)).astype(BF16)
    extra = nn(spread, labels)

    copies[1].wait()
    slot_iota = iota((slots, n), 0)
    for t in range(iters):
        target = assign_ref[t : t + 1, :]
        dest = target // owned
        local = target % owned
        rank = rank_in_bucket(iota((devices, n), 0) == dest)
        if t == 0:
            copies[2].wait()
        for h in range(CAP // ROWS):
            block = t * (CAP // ROWS) + h
            hot = onehot(slot_iota == jnp.where(rank // ROWS == h, dest * ROWS + rank % ROWS, -1))
            lane = iota((EXTRA, n), 0) - 2 * block
            digits = jnp.where(lane == 0, local // DIGIT + 1, jnp.where(lane == 1, local % DIGIT, 0))
            extra = extra + nt(hot, digits.astype(F32).astype(BF16))
            rows = nn(hot, points_ref[...]).reshape(devices, ROWS, width)
            out_ref[:, :, block * width : (block + 1) * width] = rows.astype(BF16)
    out_ref[:, :, iters * (CAP // ROWS) * width :] = extra.reshape(devices, ROWS, EXTRA).astype(BF16)


def lloyd_one_kernel(
    iters, index_ref, got_ref, centers_ref, slot_ref, coarse_hbm, out_ref, send_ref, two_ref, share_ref, scaled_ref, member_ref, sem
):
    share = share_ref.shape[0]
    start = pl.multiple_of(index_ref[0] * share, share)
    share_copy = pltpu.make_async_copy(coarse_hbm.at[pl.ds(start, share)], share_ref, sem)
    share_copy.start()
    owned, width = centers_ref.shape
    half = got_ref.shape[0] * CAP
    step = GATHER_STEP
    for t in range(iters):
        old_ref = centers_ref if t == 0 else out_ref
        rounded = old_ref[...].astype(BF16)
        mass = jnp.zeros((1, owned), F32)
        for c in range(0, half, step):
            part = got_ref.shape[0] * ROWS
            block, first = t * (CAP // ROWS) + c // part, c % part

            def rows(lo, size):
                got = got_ref[first // ROWS : (first + step) // ROWS, :, lo : lo + size]
                return got.astype(F32).reshape(step, size)

            extra = rows(iters * (CAP // ROWS) * width, EXTRA)
            values = rows(block * width, width)
            label = ((extra[:, 2 * block : 2 * block + 1] - 1.0) * DIGIT + extra[:, 2 * block + 1 : 2 * block + 2]).astype(jnp.int32)
            mask = iota((step, owned), 1) == label
            member = onehot(mask)
            member_ref[c : c + step, :] = member
            nearest = nn(member, rounded)
            distance = jnp.sum((values - nearest) ** 2, axis=1, keepdims=True) / width
            weights = 1.0 / (1.0 + distance)
            scaled_ref[c : c + step, :] = (weights * values).astype(BF16)
            mass = mass + jnp.sum(jnp.where(mask, weights, 0.0), axis=0, keepdims=True)
        scale = 1.0 / (as_column(mass) + 1.0)
        out_ref[...] = (tn(member_ref[...], scaled_ref[...]) + old_ref[...]) * scale
    rounded = out_ref[...].astype(BF16)
    slots = send_ref.shape[0]
    step = PACK_STEP
    for s in range(0, slots, step):
        pick = onehot(iota((step, owned), 0) + s == slot_ref[...])
        send_ref[s : s + step, :] = nn(pick, rounded).astype(BF16)
    member_two(got_ref, two_ref)
    share_copy.wait()


def as_column(row):
    step = 128
    diagonal = iota((step, step), 0) == iota((step, step), 1)
    parts = [
        jnp.sum(jnp.where(diagonal, row[:, c : c + step], 0.0), axis=1, keepdims=True) for c in range(0, row.shape[1], step)
    ]
    return jnp.concatenate(parts, axis=0)


def member_two(got_ref, member_ref):
    total, share = member_ref.shape
    devices = got_ref.shape[0]
    slots = devices * ROWS
    first = onehot(iota((devices, slots), 1) == iota((devices, slots), 0) * ROWS)
    extra = got_ref[:, :, got_ref.shape[2] - EXTRA :].astype(F32).reshape(slots, EXTRA)
    labels = nn(first, extra.astype(BF16)).astype(BF16)
    expand = onehot(iota((total, devices), 0) // CAP_SHARE == iota((total, devices), 1))
    labels = nn(expand, labels)
    mine = iota((total, EXTRA), 1) == CAP_SHARE + iota((total, EXTRA), 0) % CAP_SHARE
    label = jnp.sum(jnp.where(mine, labels, 0.0), axis=1, keepdims=True).astype(jnp.int32) - 1
    member_ref[...] = onehot(iota((total, share), 1) == label)


def lloyd_two_kernel(got_ref, member_ref, centers_ref, out_ref, norm_ref, weighted_ref):
    share, width = centers_ref.shape
    total = got_ref.shape[0]
    step = TWO_STEP
    centers = centers_ref[...]
    diagonal = iota((share, share), 0) == iota((share, share), 1)
    for t in range(ITER2):
        hi, lo = split2(centers)
        both = jnp.concatenate([hi, lo], axis=0)
        squares = jnp.sum(centers * centers, axis=1, keepdims=True)
        squares = jnp.sum(jnp.where(diagonal, squares, 0.0), axis=0, keepdims=True)
        mass = jnp.zeros((1, share), F32)
        for c in range(0, total, step):
            rows = got_ref[c : c + step, :]
            member = member_ref[c : c + step, :].astype(F32)
            if t == 0:
                values = rows.astype(F32)
                norm_ref[c : c + step, :] = jnp.sum(values * values, axis=1, keepdims=True)
            cross = nt(rows, both)
            cross = cross[:, :share] + cross[:, share:]
            rest = jnp.sum(member * (squares - 2.0 * cross), axis=1, keepdims=True)
            distance = jnp.maximum(norm_ref[c : c + step, :] + rest, 0.0) / width
            weights = member / (1.0 + distance)
            mass = mass + jnp.sum(weights, axis=0, keepdims=True)
            hi, lo = split2(weights)
            weighted_ref[c : c + step, :share] = hi
            weighted_ref[c : c + step, share:] = lo
        sums = tn(weighted_ref[...], got_ref[...])
        scale = 1.0 / (as_column(mass) + 1.0)
        centers = (sums[:share] + sums[share:] + centers) * scale
    out_ref[...] = centers.astype(BF16)


def place_kernel(places, groups, index_ref, *refs):
    blocks = refs[: len(places)]
    out_hbm, wide_ref, sems = refs[-3:]
    rows = blocks[0].shape[0]
    copies = []
    for i, (ref, (turn, flip)) in enumerate(zip(blocks, places)):
        wide_ref[i] = ref[...].astype(F32)
        held = lax.rem(index_ref[0] + groups - 2 * turn, groups)
        held = held + flip * (1 - 2 * lax.rem(held, 2))
        at = pl.multiple_of(held * rows, rows)
        copies.append(pltpu.make_async_copy(wide_ref.at[i], out_hbm.at[pl.ds(at, rows)], sems.at[i]))
        copies[-1].start()
    for copy in copies:
        copy.wait()


def place_first_kernel(places, groups, index_ref, fine_ref, *refs):
    fine_hbm, fine_sem = refs[len(places)], refs[-1]
    fine_copy = pltpu.make_async_copy(fine_ref, fine_hbm, fine_sem)
    fine_copy.start()
    place_kernel(places, groups, index_ref, *refs[: len(places)], *refs[len(places) + 1 : -1])
    fine_copy.wait()


def whole():
    return pl.BlockSpec(memory_space=pltpu.VMEM)


def in_hbm():
    return pl.BlockSpec(memory_space=pltpu.HBM)


def keep_in_hbm(x):
    return pltpu.with_memory_space_constraint(x, pltpu.HBM)


def params(mib):
    return pltpu.CompilerParams(vmem_limit_bytes=mib * 1024 * 1024)


def pack_points(devices, subs, owned, share, assign, parent, points):
    iters = assign.shape[0]
    return pl.pallas_call(
        lambda *refs: pack_one_kernel(devices, owned, share, subs, *refs),
        out_shape=(
            jax.ShapeDtypeStruct((devices, ROWS, iters * (CAP // ROWS) * points.shape[1] + EXTRA), BF16),
            jax.ShapeDtypeStruct(parent.shape, jnp.int32),
        ),
        in_specs=[in_hbm()] * 3,
        out_specs=(whole(), whole()),
        scratch_shapes=[
            pltpu.VMEM(assign.shape, assign.dtype),
            pltpu.VMEM(parent.shape, parent.dtype),
            pltpu.VMEM(points.shape, points.dtype),
            pltpu.SemaphoreType.DMA((3,)),
        ],
        compiler_params=params(PACK_MIB),
        name="pack_points",
    )(keep_in_hbm(assign), keep_in_hbm(parent), keep_in_hbm(points))


def level_one(iters, devices, share, index, got, centers, slot_two, coarse):
    owned, width = centers.shape
    half = devices * CAP
    slots_two = devices * CAP_SHARE
    return pl.pallas_call(
        lambda *refs: lloyd_one_kernel(iters, *refs),
        out_shape=(
            pltpu.VMEM((owned, width), F32),
            jax.ShapeDtypeStruct((slots_two, width), BF16),
            jax.ShapeDtypeStruct((slots_two, share), BF16),
            jax.ShapeDtypeStruct((share, width), F32),
        ),
        in_specs=[pl.BlockSpec(memory_space=pltpu.SMEM)] + [whole()] * 3 + [in_hbm()],
        out_specs=(whole(),) * 4,
        scratch_shapes=[
            pltpu.VMEM((half, width), BF16),
            pltpu.VMEM((half, owned), BF16),
            pltpu.SemaphoreType.DMA,
        ],
        compiler_params=params(ONE_MIB),
        name="level_one",
    )(index, got, centers, slot_two, keep_in_hbm(coarse))


def level_two(got, member, centers):
    slots, width = got.shape
    share = centers.shape[0]
    return pl.pallas_call(
        lloyd_two_kernel,
        out_shape=jax.ShapeDtypeStruct((share, width), BF16),
        in_specs=[whole()] * 3,
        out_specs=whole(),
        scratch_shapes=[
            pltpu.VMEM((slots, 1), F32),
            pltpu.VMEM((slots, 2 * share), BF16),
        ],
        compiler_params=params(TWO_MIB),
        name="level_two",
    )(got, member, centers)


def place(groups, index, blocks, out=None, fine=None):
    places, arrays = list(blocks), list(blocks.values())
    share, width = arrays[0].shape
    kernel, before, after = place_kernel, [], [out]
    out_shape, out_specs = pltpu.HBM((groups * share, width), F32), in_hbm()
    scratch = [pltpu.VMEM((len(arrays), share, width), F32), pltpu.SemaphoreType.DMA((len(arrays),))]
    if out is None:
        kernel, before, after = place_first_kernel, [fine], []
        out_shape, out_specs = (pltpu.HBM(fine.shape, F32), out_shape), (in_hbm(), in_hbm())
        scratch.append(pltpu.SemaphoreType.DMA)
    return pl.pallas_call(
        lambda *refs: kernel(places, groups, *refs),
        out_shape=out_shape,
        in_specs=[pl.BlockSpec(memory_space=pltpu.SMEM)]
        + [whole()] * (len(before) + len(arrays))
        + [in_hbm()] * len(after),
        out_specs=out_specs,
        scratch_shapes=scratch,
        input_output_aliases={1 + len(arrays): 0} if after else {},
        compiler_params=params(PLACE_MIB),
        cost_estimate=pl.CostEstimate(
            flops=len(arrays) * share * width, bytes_accessed=len(arrays) * share * width * 6, transcendentals=0
        ),
        name="place_shares",
    )(index, *before, *arrays, *after)


def gather_shares(own, groups, index, fine):
    def other_core(rows):
        return lax.ppermute(rows, "grp", [(g, g ^ 1) for g in range(groups)])

    far = [lax.ppermute(own, "grp", [(g, (g + 2 * k) % groups) for g in range(groups)]) for k in TURNS]
    fine, out = place(groups, index, {(0, 0): own}, fine=fine)
    out, own = lax.optimization_barrier((out, own))
    blocks = {(0, 1): other_core(own)}
    for k, rows in zip(TURNS, far):
        out, rows = lax.optimization_barrier((out, rows))
        blocks |= {(k, 0): rows, (k, 1): other_core(rows)}
    return fine, place(groups, index, blocks, out)


def shards(points, fine_initial, coarse_initial, assign, parent):
    groups = lax.axis_size("grp")
    subs = lax.axis_size("sub")
    devices = groups * subs
    iters = assign.shape[0]
    width = points.shape[1]
    owned = fine_initial.shape[0]
    share = coarse_initial.shape[0] // groups
    slots_two = devices * CAP_SHARE

    me = lax.axis_index("grp").astype(jnp.int32).reshape(1)
    send, slot_two = pack_points(devices, subs, owned, share, assign, parent.reshape(1, owned), points)
    send, me = lax.optimization_barrier((send, me))
    got = lax.all_to_all(send, ("grp", "sub"), split_axis=0, concat_axis=0, tiled=True)
    fine, send_two, member, centers = level_one(
        iters, devices, share, me, got, fine_initial, slot_two, coarse_initial
    )
    got_two = lax.all_to_all(
        send_two.reshape(devices, CAP_SHARE, width), ("grp", "sub"), split_axis=0, concat_axis=0, tiled=True
    ).reshape(slots_two, width)
    own = level_two(got_two, member, centers)
    return gather_shares(own, groups, me, fine)


def solution(mesh):
    return jax.shard_map(
        shards,
        mesh=mesh,
        in_specs=(
            P(("grp", "sub"), None),
            P(("grp", "sub"), None),
            P("sub", None),
            P(None, ("grp", "sub")),
            P(("grp", "sub")),
        ),
        out_specs=(P(("grp", "sub"), None), P("sub", None)),
        check_vma=False,
    )
```
